256 devices in a mesh: row: 32 (over z, y_lo, core), col: 8 (over x, y_hi).
Axes of the slice: x: 4, y: 4 (y_hi: 2, y_lo: 2; y = y_hi * 2 + y_lo), z: 8, core: 2. Of those that a mesh axis runs over, the one named last changes fastest.
Arguments:
- z_leaf: bfloat16 [524288, 512], P(('row', 'col')), may hold values from -6 to 6
- leaf_inverse: bfloat16 [2048, 256, 256], P(('row', 'col')), as said below
- lower_separator_coupling: bfloat16 [2048, 128, 256], P(('row', 'col')), may hold values from -0.375 to 0.375
- leaf_parent: int32 [2048], P(('row', 'col')), may hold values from 0 to 7
- leaf_offset: int32 [2048], P(('row', 'col')), may hold values from 0 to 1
- z_sep: bfloat16 [65536, 512], P(('row', 'col')), may hold values from -6 to 6
- sep_inverse: bfloat16 [256, 256, 256], P(('row', 'col')), as said below
- top_factor: bfloat16 [8, 8192, 8192], P('col', None, 'row'), may hold values from -0.09375 to 0.09375
- reader_mask: int32 [8, 32, 32], P('col', 'row'), may hold values 0 or 1
- z_top: bfloat16 [8, 8192, 512], P('col', 'row'), may hold values from -6 to 6
Outputs:
- y_leaf: bfloat16 [524288, 512], P(('row', 'col'))
- y_sep: bfloat16 [65536, 512], P(('row', 'col'))
- top_rhs: float32 [8, 8192, 512], P('col', 'row')
The draws below stay inside these ranges and needn't reach their ends.
Inputs may be any that keep to these rules, and one draw needn't show every extreme that they name: `leaf_inverse`: each block is lower triangular with a positive diagonal. `sep_inverse`: each block is lower triangular with a positive diagonal.
All inputs are finite; a program needn't handle non-finite values. No bound on the sum of `reader_mask` on one device may be relied on, other than what follows from the above.
Results may differ from the reference program's by a relative error of at most 0.0057.
Values may be sent and summed in bfloat16 or wider, within the bound.
No kernel may reach another device: no remote copies, remote signals or barrier semaphores. Data moves between devices by JAX's collectives and lax.ppermute only.
A program may use at most 128 MiB of HBM per device.

```python
import math
import jax
import jax.numpy as jnp
import numpy as np
from jax import lax

SAMPLES = 512
PANEL = 256
BLK = 128
TOP = 256
LEAF_DEV = 8
LEAVES = 2048
SEPS = 256
N_ROW = 32
N_COL = 8


def lower_blocks(key, count, order):
    first_key, second_key = jax.random.split(key)
    spread = jax.random.normal(first_key, (count, order, order), jnp.float32)
    diagonal = jnp.exp(jax.random.uniform(second_key, (count, order, 1), jnp.float32, -0.7, 0.7))
    rows = jnp.arange(order, dtype=jnp.int32)[:, None]
    cols = jnp.arange(order, dtype=jnp.int32)[None, :]
    strict = (cols < rows).astype(jnp.float32)
    identity = (cols == rows).astype(jnp.float32)
    scaled = spread * (0.6 / order ** 0.5)
    return scaled * strict * diagonal + identity * diagonal


def draw_leaf_inverse(key, part):
    return lower_blocks(jax.random.fold_in(key, 11), LEAVES, PANEL).astype(jnp.bfloat16)


def draw_sep_inverse(key, part):
    return lower_blocks(jax.random.fold_in(key, 23), SEPS, PANEL).astype(jnp.bfloat16)


def plant(values, own_key, low, high):
    shape = values.shape
    index_at = [jax.random.randint(jax.random.fold_in(own_key, axis), (), 0, shape[axis]) for axis in range(len(shape))]
    values = values.at[tuple(index_at)].set(low)
    longest = shape.index(max(shape))
    index_at[longest] = (index_at[longest] + 1) % shape[longest]
    return values.at[tuple(index_at)].set(high)


def block_scale(own_key, extent, shards, least, high):
    loudness = 1.0
    for axis_at, shards_of in shards:
        steps = jax.random.uniform(jax.random.fold_in(jax.random.fold_in(own_key, 6), axis_at), (shards_of,), jnp.float32, least / len(shards), high / len(shards))
        loudness = loudness * jnp.repeat(jnp.exp(steps), extent[axis_at] // shards_of).reshape((-1,) + (1,) * (len(extent) - 1 - axis_at))
    return loudness


def rank_bounds(number_of, skew):
    weights = [(1 << 20) // math.isqrt(rank ** skew) + 1 for rank in range(1, number_of + 1)]
    deviation = 1 + sum(weights) // (1 << 30)
    return np.cumsum(np.array([max(1, weight // deviation) for weight in weights]))


def skewed_ids(stream_key, dims, amount, lean):
    table = rank_bounds(amount, lean)
    ticket = jax.random.randint(jax.random.fold_in(stream_key, 1), dims, 0, int(table[amount - 1]))
    rank = jnp.searchsorted(jnp.asarray(table, jnp.int32), ticket, side="right")
    return jax.random.permutation(jax.random.fold_in(stream_key, 2), amount)[rank].astype(jnp.int32)


def noise(rng, shape, deviation, reach, shards=(), kind=jnp.bfloat16):
    factor_of = block_scale(rng, shape, shards, -0.22, 0.18) if shards else 1.0
    values = jax.random.normal(rng, shape, jnp.float32) * deviation * factor_of
    return jnp.minimum(jnp.maximum(values, -reach), reach).astype(kind)


def setup_inputs(seed: int = 0) -> dict:
    arg_keys = jax.random.split(jax.random.key(seed), 11)
    return {
        "z_leaf": noise(arg_keys[0], (LEAVES * PANEL, SAMPLES), 1.0, 6.0, ((0, 256),)),
        "leaf_inverse": draw_leaf_inverse(jax.random.fold_in(arg_keys[10], 71), 0),
        "lower_separator_coupling": noise(arg_keys[2], (LEAVES, BLK, PANEL), PANEL ** -0.5, 0.375, ((0, 256),)),
        "leaf_parent": plant(skewed_ids(arg_keys[3], (LEAVES,), N_COL, 2), jax.random.fold_in(arg_keys[3], 3), 0, N_COL - 1).astype(jnp.int32),
        "leaf_offset": plant(jax.random.randint(arg_keys[4], (LEAVES,), 0, 2), jax.random.fold_in(arg_keys[4], 1), 0, 1).astype(jnp.int32),
        "z_sep": noise(arg_keys[5], (SEPS * PANEL, SAMPLES), 1.0, 6.0, ((0, 256),)),
        "sep_inverse": draw_sep_inverse(jax.random.fold_in(arg_keys[10], 71), 0),
        "top_factor": noise(arg_keys[7], (N_COL, N_ROW * TOP, N_ROW * PANEL), (N_ROW * PANEL // 2) ** -0.5, 0.09375, ((0, 8), (2, 32))),
        "reader_mask": plant((jax.random.randint(arg_keys[8], (N_COL, N_ROW, N_ROW), 0, 2) < 1).astype(jnp.int32), jax.random.fold_in(arg_keys[8], 1), 0, 1),
        "z_top": noise(arg_keys[9], (N_COL, N_ROW * TOP, SAMPLES), 1.0, 6.0, ((0, 8), (1, 32))),
    }


def reference(z_leaf, leaf_inverse, lower_separator_coupling, leaf_parent, leaf_offset, z_sep, sep_inverse, top_factor, reader_mask, z_top):
    leaf_rhs = z_leaf.reshape(LEAVES, PANEL, SAMPLES).astype(jnp.float32)
    solution_rows = jnp.einsum("lij,ljs->lis", leaf_inverse.astype(jnp.float32), leaf_rhs).astype(jnp.bfloat16)
    panel_share = jnp.einsum("qxw,qwo->qxo", lower_separator_coupling.astype(jnp.float32), solution_rows.astype(jnp.float32))
    leaf_ids = jnp.arange(LEAVES, dtype=jnp.int32)
    row_index = (leaf_ids // LEAF_DEV) // N_COL
    dest_block = ((row_index * N_COL + leaf_parent) * 2 + leaf_offset).astype(jnp.int32)
    update = jax.ops.segment_sum(panel_share, dest_block, num_segments=2 * SEPS)
    update = update.reshape(SEPS * PANEL, SAMPLES)
    reduced = (z_sep.astype(jnp.float32) - update).astype(jnp.bfloat16)
    sep_solved = jnp.einsum("sij,sjk->sik", sep_inverse.astype(jnp.float32), reduced.reshape(SEPS, PANEL, SAMPLES).astype(jnp.float32)).astype(jnp.bfloat16)
    sep_panels = sep_solved.reshape(N_ROW, N_COL, PANEL, SAMPLES).transpose(1, 0, 2, 3).reshape(N_COL, N_ROW * PANEL, SAMPLES)
    readers = reader_mask.astype(jnp.bfloat16).transpose(0, 2, 1)

    def one_column(inputs):
        factor, mask_rows, panel_stack, rhs_top = inputs
        masked = (factor.reshape(N_ROW, TOP, N_ROW, PANEL) * mask_rows[:, None, :, None]).reshape(N_ROW * TOP, N_ROW * PANEL)
        summed = jnp.dot(masked, panel_stack, preferred_element_type=jnp.float32)
        return rhs_top.astype(jnp.float32) - summed

    top_rhs = lax.map(one_column, (top_factor, readers, sep_panels, z_top))
    return solution_rows.reshape(LEAVES * PANEL, SAMPLES), sep_solved.reshape(SEPS * PANEL, SAMPLES), top_rhs
```

```python
import functools

import jax
import jax.numpy as jnp
from jax import lax
from jax.experimental import pallas as pl
from jax.experimental.pallas import tpu as pltpu
from jax.sharding import PartitionSpec as P

BF = jnp.bfloat16
F32 = jnp.float32
CHUNKS = 2
PARTS = ((0, 3), (3, 8))


def swap(x, bits):
    n = lax.axis_size("row")
    return lax.ppermute(x, "row", [(i, i ^ bits) for i in range(n)])


def chain(x):
    n = lax.axis_size("row")
    return lax.ppermute(x, "row", [(i, (i + (4 if i % 2 == 0 else n - 4)) % n) for i in range(n)])


def leaf_kernel(parent, offset, z_ref, inv_ref, coup_ref, y_ref, out_ref, acc):
    step = pl.program_id(0)

    @pl.when(step == 0)
    def _():
        acc[...] = jnp.zeros_like(acc)

    y = jnp.dot(inv_ref[0], z_ref[...], preferred_element_type=F32).astype(BF)
    y_ref[...] = y
    share = jnp.dot(coup_ref[0], y, preferred_element_type=F32)
    target = parent[step] * 2 + offset[step]
    acc[target] += share

    @pl.when(step == pl.num_programs(0) - 1)
    def _():
        out_ref[...] = acc[...].astype(BF)


def leaf_solve(z_leaf, leaf_inverse, coupling, parent, offset, targets):
    count, rows, _ = leaf_inverse.shape
    blk = coupling.shape[1]
    samples = z_leaf.shape[1]
    return pl.pallas_call(
        leaf_kernel,
        grid_spec=pltpu.PrefetchScalarGridSpec(
            num_scalar_prefetch=2,
            grid=(count,),
            in_specs=[
                pl.BlockSpec((rows, samples), lambda i, *_: (i, 0)),
                pl.BlockSpec((1, rows, rows), lambda i, *_: (i, 0, 0)),
                pl.BlockSpec((1, blk, rows), lambda i, *_: (i, 0, 0)),
            ],
            out_specs=[
                pl.BlockSpec((rows, samples), lambda i, *_: (i, 0)),
                pl.BlockSpec((targets, blk, samples), lambda i, *_: (0, 0, 0)),
            ],
            scratch_shapes=[pltpu.VMEM((targets, blk, samples), F32)],
        ),
        out_shape=[
            jax.ShapeDtypeStruct((count * rows, samples), BF),
            jax.ShapeDtypeStruct((targets, blk, samples), BF),
        ],
        compiler_params=pltpu.CompilerParams(vmem_limit_bytes=32 << 20),
        cost_estimate=pl.CostEstimate(flops=810_000_000, bytes_accessed=8 << 20, transcendentals=0),
        name="leaf_solve",
    )(parent, offset, z_leaf, leaf_inverse, coupling)


def pick_kernel(first, table, mask, *refs):
    step = pl.program_id(0)
    for m in range(4):
        keep = mask[table[m * 8 + first + step]].astype(F32)
        refs[4 + m][...] = (refs[m][...].astype(F32) * keep).astype(BF)


def pick(factor, table, mask, first, last):
    def spec(m):
        return pl.BlockSpec((256, 256), lambda i, table, mask: (table[m * 8 + first + i], 0))

    rows = (last - first) * 256
    return pl.pallas_call(
        functools.partial(pick_kernel, first),
        grid_spec=pltpu.PrefetchScalarGridSpec(
            num_scalar_prefetch=2,
            grid=(last - first,),
            in_specs=[spec(m) for m in range(4)],
            out_specs=[pl.BlockSpec((256, 256), lambda i, *_: (i, 0))] * 4,
        ),
        out_shape=[jax.ShapeDtypeStruct((rows, 256), BF)] * 4,
        compiler_params=pltpu.CompilerParams(vmem_limit_bytes=32 << 20),
        cost_estimate=pl.CostEstimate(flops=rows * 1024, bytes_accessed=rows * 4096, transcendentals=0),
        name="pick_factor",
    )(table, mask, factor, factor, factor, factor)


def sep_kernel(recv_ref, z_ref, inv_ref, y_ref):
    total = recv_ref[0].astype(F32)
    for i in range(1, recv_ref.shape[0]):
        total += recv_ref[i].astype(F32)
    reduced = (z_ref[...].astype(F32) - total).astype(BF)
    y_ref[...] = jnp.dot(inv_ref[0], reduced, preferred_element_type=F32).astype(BF)


def sep_solve(recv, z_sep, sep_inverse):
    count, rows, samples = recv.shape
    width = 128
    return pl.pallas_call(
        sep_kernel,
        grid=(samples // width,),
        in_specs=[
            pl.BlockSpec((count, rows, width), lambda i: (0, 0, i)),
            pl.BlockSpec((rows, width), lambda i: (0, i)),
            pl.BlockSpec((1, rows, rows), lambda i: (0, 0, 0)),
        ],
        out_specs=pl.BlockSpec((rows, width), lambda i: (0, i)),
        out_shape=jax.ShapeDtypeStruct((rows, samples), BF),
        compiler_params=pltpu.CompilerParams(vmem_limit_bytes=32 << 20),
        cost_estimate=pl.CostEstimate(flops=70_000_000, bytes_accessed=3 << 20, transcendentals=0),
        name="sep_solve",
    )(recv, z_sep, sep_inverse)


def stage_kernel(has_recv, add_first, final, core, *refs):
    f = refs[0:4]
    y = refs[4:8]
    total = jnp.dot(f[0][...], y[0][...], preferred_element_type=F32)
    for m in range(1, 4):
        total += jnp.dot(f[m][...], y[m][...], preferred_element_type=F32)
    if has_recv:
        recv = refs[8][...].astype(F32)
        if add_first:
            recv = jnp.where(pl.program_id(0) == core[0], recv, 0.0)
        total += recv
    if final:
        total = refs[10][...].astype(F32) - (total + refs[9][...].astype(F32))
    refs[-1][...] = total.astype(refs[-1].dtype)


def stage(core, factors, first, blocks, panels, chunk, width, recv=None, final=None):
    add_first = recv is not None and final is None and recv.shape[0] == 256
    specs = [pl.BlockSpec((256, 256), lambda i, c: (first + i, 0))] * 4
    specs += [pl.BlockSpec((256, width), lambda i, c: (0, chunk))] * 4
    args = list(factors) + list(panels)
    if recv is not None:
        if add_first:
            specs.append(pl.BlockSpec((256, width), lambda i, c: (0, 0)))
        elif final is not None:
            specs.append(pl.BlockSpec((256, width), lambda i, c: (c[0], 0)))
        else:
            specs.append(pl.BlockSpec((256, width), lambda i, c: (i, 0)))
        args.append(recv)
    dtype = BF
    if final is not None:
        other, z_top = final
        specs.append(pl.BlockSpec((256, width), lambda i, c: (0, 0)))
        specs.append(pl.BlockSpec((256, width), lambda i, c: (0, chunk)))
        args += [other, z_top]
        dtype = F32
    rows = blocks * 256
    return pl.pallas_call(
        functools.partial(stage_kernel, recv is not None, add_first, final is not None),
        grid_spec=pltpu.PrefetchScalarGridSpec(
            num_scalar_prefetch=1,
            grid=(blocks,),
            in_specs=specs,
            out_specs=pl.BlockSpec((256, width), lambda i, c: (i, 0)),
        ),
        out_shape=jax.ShapeDtypeStruct((rows, width), dtype),
        compiler_params=pltpu.CompilerParams(vmem_limit_bytes=32 << 20),
        cost_estimate=pl.CostEstimate(
            flops=rows * 2048 * width, bytes_accessed=rows * 2048 + 2048 * width, transcendentals=0
        ),
        name="stage",
    )(core, *args)


def shards(
    z_leaf,
    leaf_inverse,
    lower_separator_coupling,
    leaf_parent,
    leaf_offset,
    z_sep,
    sep_inverse,
    top_factor,
    reader_mask,
    z_top,
):
    columns = lax.axis_size("col")
    samples = z_sep.shape[1]
    me = lax.axis_index("row").astype(jnp.int32)
    core = me % 2
    table = []
    for m in range(4):
        peer = me ^ m
        sign = 1 - 2 * (peer % 2)
        base = me // 4
        pair = (peer // 2) % 2
        side = peer % 2

        def block(z, k):
            return ((z + 16) % 8) * 4 + pair * 2 + k

        table.append(block(base + 4, side))
        for d in (3, 2, 1):
            for k in (0, 1):
                table.append(block(base + d * sign, k))
        table.append(block(base, side))
    table = jnp.stack(table).astype(jnp.int32)
    mask = reader_mask[0, 0]

    y_leaf, blocks = leaf_solve(
        z_leaf, leaf_inverse, lower_separator_coupling, leaf_parent, leaf_offset, 2 * columns
    )
    sent = blocks.reshape(columns, 256, samples)
    recv = lax.all_to_all(sent, "col", split_axis=0, concat_axis=0, tiled=True)
    factors = []
    for first, last in PARTS:
        own = pick(top_factor[0], table, mask, first, last)
        factors.append([own[0]] + [swap(own[m], m) for m in (2, 3, 1)])
    factors = [[f[0], f[3], f[1], f[2]] for f in factors]
    y_sep = sep_solve(recv, z_sep, sep_inverse)
    y_pair = swap(y_sep, 2)
    y_core = swap(y_sep, 1)
    y_diag = swap(y_pair, 1)
    panels = [y_sep, y_core, y_pair, y_diag]

    core_id = core.reshape(1)
    width = samples // CHUNKS

    def where(j):
        for part, (first, last) in enumerate(PARTS):
            if first <= j < last:
                return factors[part], j - first

    held = [None] * CHUNKS
    for j, count in ((0, 1), (1, 2), (3, 2), (5, 2)):
        for c in range(CHUNKS):
            f, first = where(j)
            held[c] = chain(stage(core_id, f, first, count, panels, c, width, recv=held[c]))
    tops = []
    for c in range(CHUNKS):
        away = lax.dynamic_slice_in_dim(held[c], (1 - core) * 256, 256, axis=0)
        other = swap(away, 1)
        f, first = where(7)
        tops.append(stage(core_id, f, first, 1, panels, c, width, recv=held[c], final=(other, z_top[0])))
    top_rhs = jnp.concatenate(tops, axis=1)
    return y_leaf, y_sep, top_rhs[None]


def solution(mesh):
    return jax.shard_map(
        shards,
        mesh=mesh,
        in_specs=(
            P(("row", "col"), None),
            P(("row", "col"), None, None),
            P(("row", "col"), None, None),
            P(("row", "col")),
            P(("row", "col")),
            P(("row", "col"), None),
            P(("row", "col"), None, None),
            P("col", None, "row"),
            P("col", "row", None),
            P("col", "row", None),
        ),
        out_specs=(P(("row", "col"), None), P(("row", "col"), None), P("col", "row", None)),
        check_vma=False,
    )
```

```python
import functools

import jax
import jax.numpy as jnp
from jax import lax
from jax.experimental import pallas as pl
from jax.experimental.pallas import tpu as pltpu
from jax.sharding import PartitionSpec as P

BF = jnp.bfloat16
F32 = jnp.float32
CHUNKS = 2
SPLIT = 5


def swap(x, bits):
    n = lax.axis_size("row")
    return lax.ppermute(x, "row", [(i, i ^ bits) for i in range(n)])


def chain(x, chips=1, cross=0):
    n = lax.axis_size("row")
    hop = 4 * chips
    return lax.ppermute(
        x, "row", [(i, ((i + (hop if i % 2 == 0 else n - hop)) % n) ^ cross) for i in range(n)]
    )


def across(x, step, cross=0):
    n = lax.axis_size("col")
    return lax.ppermute(x, "col", [(i, ((i + 2 * step) % n) ^ cross) for i in range(n)])


def diagonal(x):
    rows, cols = lax.axis_size("row"), lax.axis_size("col")
    return lax.ppermute(
        x, ("row", "col"), [(r * cols + c, (r ^ 2) * cols + (c ^ 1)) for r in range(rows) for c in range(cols)]
    )


def leaf_kernel(place, parent, offset, z_ref, inv_ref, coup_ref, y_ref, *refs):
    up2, down2, up0, up1, down0, down1, own, z, inv, coup, y, acc, in_sem, out_sem = refs
    count = inv.shape[0]
    reads, writes = [], []
    for i in range(count):
        rows = pl.ds(i * 256, 256)
        reads.append(
            [
                pltpu.make_async_copy(inv_ref.at[i], inv.at[i], in_sem.at[3 * i]),
                pltpu.make_async_copy(z_ref.at[rows, :], z.at[rows, :], in_sem.at[3 * i + 1]),
                pltpu.make_async_copy(coup_ref.at[i], coup.at[i], in_sem.at[3 * i + 2]),
            ]
        )
        for copy in reads[i]:
            copy.start()
    acc[...] = jnp.zeros_like(acc)
    for i in range(count):
        for copy in reads[i]:
            copy.wait()
        rows = slice(i * 256, i * 256 + 256)
        solved = jnp.dot(inv[i], z[rows, :], preferred_element_type=F32).astype(BF)
        y[rows, :] = solved
        writes.append(
            pltpu.make_async_copy(
                y.at[pl.ds(i * 256, 256), :], y_ref.at[pl.ds(i * 256, 256), :], out_sem.at[i]
            )
        )
        writes[i].start()
        p = parent[i]
        away = ((p >> 1) - place[1]) & 3
        side = (p & 1) ^ place[2]
        acc[(away * 2 + offset[i]) * 2 + side] += jnp.dot(coup[i], solved, preferred_element_type=F32)
    up2[...] = acc[8:10].astype(BF)
    down2[...] = acc[10:12].astype(BF)
    own[...] = acc[0:4]
    up0[...] = acc[4:6].astype(BF)
    up1[...] = acc[6:8].astype(BF)
    down0[...] = acc[12:14].astype(BF)
    down1[...] = acc[14:16].astype(BF)
    for copy in writes:
        copy.wait()


def leaf_solve(place, z_leaf, leaf_inverse, coupling, parent, offset, targets):
    count, rows, _ = leaf_inverse.shape
    blk = coupling.shape[1]
    samples = z_leaf.shape[1]
    return pl.pallas_call(
        leaf_kernel,
        grid_spec=pltpu.PrefetchScalarGridSpec(
            num_scalar_prefetch=3,
            grid=(1,),
            in_specs=[pl.BlockSpec(memory_space=pl.ANY)] * 3,
            out_specs=[pl.BlockSpec(memory_space=pl.ANY)]
            + [pl.BlockSpec((2, blk, samples), lambda i, *_: (0, 0, 0))] * 6
            + [pl.BlockSpec((4, blk, samples), lambda i, *_: (0, 0, 0))],
            scratch_shapes=[
                pltpu.VMEM(z_leaf.shape, BF),
                pltpu.VMEM(leaf_inverse.shape, BF),
                pltpu.VMEM(coupling.shape, BF),
                pltpu.VMEM(z_leaf.shape, BF),
                pltpu.VMEM((targets, blk, samples), F32),
                pltpu.SemaphoreType.DMA((3 * count,)),
                pltpu.SemaphoreType.DMA((count,)),
            ],
        ),
        out_shape=[jax.ShapeDtypeStruct((count * rows, samples), BF)]
        + [jax.ShapeDtypeStruct((2, blk, samples), BF)] * 6
        + [jax.ShapeDtypeStruct((4, blk, samples), F32)],
        compiler_params=pltpu.CompilerParams(vmem_limit_bytes=24 << 20),
        cost_estimate=pl.CostEstimate(flops=810_000_000, bytes_accessed=8 << 20, transcendentals=0),
        name="leaf_solve",
    )(place, parent, offset, z_leaf, leaf_inverse, coupling)


def gather_kernel(own, from0, from1, back0, back1, z_ref, part_ref, mine_ref, rest_ref):
    for b, (f, g) in enumerate(((from0, back0), (from1, back1))):
        rows = slice(b * 128, b * 128 + 128)
        rest = z_ref[rows, :].astype(F32) - (own[2 * b] + f[0].astype(F32) + g[0].astype(F32))
        rest_ref[rows, :] = rest
        mine_ref[rows, :] = rest.astype(BF)
        part_ref[rows, :] = (own[2 * b + 1] + f[1].astype(F32) + g[1].astype(F32)).astype(BF)


def gather_x(own, from0, from1, back0, back1, z_sep):
    shape = z_sep.shape
    return pl.pallas_call(
        gather_kernel,
        out_shape=[
            jax.ShapeDtypeStruct(shape, BF),
            jax.ShapeDtypeStruct(shape, BF),
            jax.ShapeDtypeStruct(shape, F32),
        ],
        compiler_params=pltpu.CompilerParams(vmem_limit_bytes=16 << 20),
        cost_estimate=pl.CostEstimate(flops=2_000_000, bytes_accessed=4 << 20, transcendentals=0),
        name="gather_x",
    )(own, from0, from1, back0, back1, z_sep)


def block_of(me, m, j):
    peer = me ^ m
    z, pair, side = peer >> 2, (peer >> 1) & 1, peer & 1
    sign = 1 - 2 * side
    if j == 0:
        z, side = z + 4, side
    elif j < 7:
        z, side = z + sign * (3 - (j - 1) // 2), (j - 1) % 2
    return ((z + 8) & 7) * 4 + pair * 2 + side


def pick_kernel(wanted, place, mask, factor, extra, *refs):
    outs = refs[: len(wanted)]
    held, in_sem, out_sem = refs[len(wanted) :]
    jobs = []
    for o, groups in enumerate(wanted):
        order = [(m, j) for m, lo, hi in groups for j in range(lo, hi)]
        jobs += [(o, m, j, at) for at, (m, j) in enumerate(order)]
    reads, writes = [], []
    for i, (o, m, j, at) in enumerate(jobs):
        block = pl.multiple_of(block_of(place[0], m, j) * 256, 256)
        reads.append(pltpu.make_async_copy(factor.at[pl.ds(block, 256), :], held.at[i], in_sem.at[i]))
        reads[-1].start()
    if extra is not None:
        tail = outs[-1].shape[0] - 256
        reads.append(pltpu.make_async_copy(extra, held.at[len(jobs)], in_sem.at[len(jobs)]))
        reads[-1].start()
    for i, (o, m, j, at) in enumerate(jobs):
        reads[i].wait()
        keep = mask[block_of(place[0], m, j)].astype(F32)
        held[i] = (held[i].astype(F32) * keep).astype(BF)
        writes.append(
            pltpu.make_async_copy(held.at[i], outs[o].at[pl.ds(at * 256, 256), :], out_sem.at[i])
        )
        writes[-1].start()
    if extra is not None:
        reads[-1].wait()
        writes.append(
            pltpu.make_async_copy(held.at[len(jobs)], outs[-1].at[pl.ds(tail, 256), :], out_sem.at[len(jobs)])
        )
        writes[-1].start()
    for copy in writes:
        copy.wait()


def pick(place, mask, factor, wanted, limit, extra=None):
    sizes = [sum(hi - lo for _, lo, hi in groups) for groups in wanted]
    total = sum(sizes)
    kernel = functools.partial(pick_kernel, wanted)
    args = [factor]
    if extra is None:
        kernel = lambda place, mask, factor, *refs: pick_kernel(wanted, place, mask, factor, None, *refs)
    else:
        sizes[-1] += 1
        args.append(extra)
    return pl.pallas_call(
        kernel,
        grid_spec=pltpu.PrefetchScalarGridSpec(
            num_scalar_prefetch=2,
            grid=(1,),
            in_specs=[pl.BlockSpec(memory_space=pl.ANY)] * len(args),
            out_specs=[pl.BlockSpec(memory_space=pl.ANY)] * len(wanted),
            scratch_shapes=[
                pltpu.VMEM((total + 1, 256, 256), BF),
                pltpu.SemaphoreType.DMA((total + 1,)),
                pltpu.SemaphoreType.DMA((total + 1,)),
            ],
        ),
        out_shape=[jax.ShapeDtypeStruct((size * 256, 256), BF) for size in sizes],
        compiler_params=pltpu.CompilerParams(vmem_limit_bytes=limit),
        cost_estimate=pl.CostEstimate(flops=total << 16, bytes_accessed=total << 18, transcendentals=0),
        name="pick_factor",
    )(place, mask, *args)


def sep_kernel(rest_ref, part_ref, near_ref, cross_ref, inv_ref, near_inv_ref, y_ref, pair_ref):
    mine = (rest_ref[...] - part_ref[...].astype(F32)).astype(BF)
    y = jnp.dot(inv_ref[0], mine, preferred_element_type=F32).astype(BF)
    y_ref[...] = y
    near = (near_ref[...].astype(F32) - cross_ref[...].astype(F32)).astype(BF)
    pair_ref[0:256, :] = y
    pair_ref[256:512, :] = jnp.dot(near_inv_ref[...], near, preferred_element_type=F32).astype(BF)


def sep_solve(rest, part, near, cross, sep_inverse, far_f):
    rows, samples = rest.shape
    whole = pl.BlockSpec((rows, samples), lambda i: (0, 0))
    last = far_f.shape[0] // rows - 1
    return pl.pallas_call(
        sep_kernel,
        grid=(1,),
        in_specs=[whole] * 4
        + [
            pl.BlockSpec((1, rows, rows), lambda i: (0, 0, 0)),
            pl.BlockSpec((rows, rows), lambda i: (last, 0)),
        ],
        out_specs=[whole, pl.BlockSpec((2 * rows, samples), lambda i: (0, 0))],
        out_shape=[
            jax.ShapeDtypeStruct((rows, samples), BF),
            jax.ShapeDtypeStruct((2 * rows, samples), BF),
        ],
        compiler_params=pltpu.CompilerParams(vmem_limit_bytes=16 << 20),
        cost_estimate=pl.CostEstimate(flops=140_000_000, bytes_accessed=2 << 20, transcendentals=0),
        name="sep_solve",
    )(rest, part, near, cross, sep_inverse, far_f)


def multiply(f, y):
    total = jnp.dot(f[0][...], y[0][...], preferred_element_type=F32)
    for m in range(1, 4):
        total += jnp.dot(f[m][...], y[m][...], preferred_element_type=F32)
    return total


def start_kernel(*refs):
    refs[8][...] = multiply(refs[0:4], refs[4:8]).astype(BF)


def start(factors, first, blocks, panels, chunk, width):
    return pl.pallas_call(
        start_kernel,
        grid=(blocks,),
        in_specs=[pl.BlockSpec((256, 256), lambda i: (first + i, 0))] * 4
        + [pl.BlockSpec((256, width), lambda i, m=m: (m // 2, chunk)) for m in range(4)],
        out_specs=pl.BlockSpec((256, width), lambda i: (i, 0)),
        out_shape=jax.ShapeDtypeStruct((256 * blocks, width), BF),
        compiler_params=pltpu.CompilerParams(vmem_limit_bytes=16 << 20),
        cost_estimate=pl.CostEstimate(flops=blocks * 512 * 1024 * width, bytes_accessed=3 << 20, transcendentals=0),
        name="chain_start",
    )(*factors, *panels)


def middle_kernel(core, *refs):
    total = multiply(refs[0:4], refs[4:8]) + refs[8][...].astype(F32)
    total += jnp.where(pl.program_id(0) == core[0], refs[9][...].astype(F32), 0.0)
    refs[10][...] = total.astype(BF)


def middle(core, factors, first, panels, chunk, width, near, far):
    return pl.pallas_call(
        middle_kernel,
        grid_spec=pltpu.PrefetchScalarGridSpec(
            num_scalar_prefetch=1,
            grid=(2,),
            in_specs=[pl.BlockSpec((256, 256), lambda i, c: (first + i, 0))] * 4
            + [pl.BlockSpec((256, width), lambda i, c, m=m: (m // 2, chunk)) for m in range(4)]
            + [
                pl.BlockSpec((256, width), lambda i, c: (i, 0)),
                pl.BlockSpec((256, width), lambda i, c: (0, chunk)),
            ],
            out_specs=pl.BlockSpec((256, width), lambda i, c: (i, 0)),
        ),
        out_shape=jax.ShapeDtypeStruct((512, width), BF),
        compiler_params=pltpu.CompilerParams(vmem_limit_bytes=16 << 20),
        cost_estimate=pl.CostEstimate(flops=1024 * 1024 * width, bytes_accessed=3 << 20, transcendentals=0),
        name="chain_middle",
    )(core, *factors, *panels, near, far)


def last_kernel(core, *refs):
    total = (multiply(refs[0:4], refs[4:8]) + refs[8][...].astype(F32)).astype(BF)

    @pl.when(pl.program_id(0) == 0)
    def _():
        refs[9][...] = total

    @pl.when(pl.program_id(0) == 1)
    def _():
        refs[10][...] = total


def last(core, factors, first, panels, chunk, width, recv):
    return pl.pallas_call(
        last_kernel,
        grid_spec=pltpu.PrefetchScalarGridSpec(
            num_scalar_prefetch=1,
            grid=(2,),
            in_specs=[pl.BlockSpec((256, 256), lambda i, c, k=k: (k + (c[0] ^ i), 0)) for k in first]
            + [pl.BlockSpec((256, width), lambda i, c, m=m: (m // 2, chunk)) for m in range(4)]
            + [pl.BlockSpec((256, width), lambda i, c: (c[0] ^ i, 0))],
            out_specs=[pl.BlockSpec((256, width), lambda i, c: (0, 0))] * 2,
        ),
        out_shape=[jax.ShapeDtypeStruct((256, width), BF)] * 2,
        compiler_params=pltpu.CompilerParams(vmem_limit_bytes=16 << 20),
        cost_estimate=pl.CostEstimate(flops=1024 * 1024 * width, bytes_accessed=3 << 20, transcendentals=0),
        name="chain_last",
    )(core, *factors, *panels, recv)


def own_kernel(*refs):
    refs[9][...] = refs[8][...].astype(F32) - multiply(refs[0:4], refs[4:8])


def own_rows(factors, first, panels, z_top):
    samples = z_top.shape[1]
    return pl.pallas_call(
        own_kernel,
        grid=(1,),
        in_specs=[pl.BlockSpec((256, 256), lambda i, k=k: (k, 0)) for k in first]
        + [pl.BlockSpec((256, samples), lambda i, m=m: (m // 2, 0)) for m in range(4)]
        + [pl.BlockSpec((256, samples), lambda i: (0, 0))],
        out_specs=pl.BlockSpec((256, samples), lambda i: (0, 0)),
        out_shape=jax.ShapeDtypeStruct((256, samples), F32),
        compiler_params=pltpu.CompilerParams(vmem_limit_bytes=16 << 20),
        cost_estimate=pl.CostEstimate(flops=512 * 1024 * samples, bytes_accessed=3 << 20, transcendentals=0),
        name="own_rows",
    )(*factors, *panels, z_top)


def shards(
    z_leaf,
    leaf_inverse,
    lower_separator_coupling,
    leaf_parent,
    leaf_offset,
    z_sep,
    sep_inverse,
    top_factor,
    reader_mask,
    z_top,
):
    columns = lax.axis_size("col")
    samples = z_sep.shape[1]
    me = lax.axis_index("row").astype(jnp.int32)
    col = lax.axis_index("col").astype(jnp.int32)
    core = me & 1
    place = jnp.stack([me, col >> 1, col & 1])
    mask = reader_mask[0, 0]

    near_f, far_a = pick(
        place, mask, top_factor[0], (((1, 0, 8),), ((2, 0, SPLIT), (3, 0, SPLIT))), 60 << 20, sep_inverse[0]
    )
    far_a = swap(far_a, 2)
    z_leaf, near_f = lax.optimization_barrier((z_leaf, near_f))
    near_f = swap(near_f, 1)
    y_leaf, up2, down2, up0, up1, down0, down1, own = leaf_solve(
        place, z_leaf, leaf_inverse, lower_separator_coupling, leaf_parent, leaf_offset, 2 * columns
    )
    from2, back2 = across(up2, 1), across(down2, 3)
    from1, back0 = across(up1, 1), across(down0, 3)
    own_f, far_b, cross_b = pick(
        place, mask, top_factor[0], (((0, 0, 8),), ((2, SPLIT, 8),), ((3, SPLIT, 8),)), 16 << 20)
    from1, near_f, far_a, own_f, far_b, cross_b = lax.optimization_barrier(
        (from1, near_f, far_a, own_f, far_b, cross_b)
    )
    cross_a = swap(far_a[SPLIT * 256 : 2 * SPLIT * 256], 1)
    near_inverse = far_a[2 * SPLIT * 256 :]
    from0 = across((up0.astype(F32) + from2.astype(F32)).astype(BF), 1)
    back1 = across((down1.astype(F32) + back2.astype(F32)).astype(BF), 3)
    part, mine, rest = gather_x(own, from0, from1, back0, back1, z_sep)
    theirs, cross, near = across(part, 0, 1), diagonal(part), swap(mine, 2)
    y_sep, pair = sep_solve(rest, theirs, near, cross, sep_inverse, near_inverse)
    pair_core = swap(pair, 1)
    pair_core, far_b, cross_b = lax.optimization_barrier((pair_core, far_b, cross_b))
    far_b, cross_b = swap(far_b, 2), swap(cross_b, 3)
    panels = [pair, pair_core, pair, pair_core]
    first_f = [own_f, near_f, far_a, cross_a]
    skip = (SPLIT, SPLIT, 0, 0)

    core_id = core.reshape(1)
    width = samples // CHUNKS
    far = chain(start(first_f, 0, 1, panels, 0, samples), 2)
    arrived = [chain(start(first_f, 1, 2, panels, c, width)) for c in range(CHUNKS)]
    sums = [middle(core_id, first_f, 3, panels, c, width, arrived[c], far) for c in range(CHUNKS)]
    last_f = [own_f, near_f, far_b, cross_b]
    arrived = [chain(x) for x in sums]
    for c in range(CHUNKS):
        same, other = last(core_id, last_f, skip, panels, c, width, arrived[c])
        arrived[c] = (chain(same), chain(other, 1, 1))
    rest = own_rows(last_f, [k + 2 for k in skip], panels, z_top[0])
    tops = [
        rest[:, c * width : (c + 1) * width] - (arrived[c][0].astype(F32) + arrived[c][1].astype(F32))
        for c in range(CHUNKS)
    ]
    top_rhs = jnp.concatenate(tops, axis=1)
    return y_leaf, y_sep, top_rhs[None]


def solution(mesh):
    return jax.shard_map(
        shards,
        mesh=mesh,
        in_specs=(
            P(("row", "col"), None),
            P(("row", "col"), None, None),
            P(("row", "col"), None, None),
            P(("row", "col")),
            P(("row", "col")),
            P(("row", "col"), None),
            P(("row", "col"), None, None),
            P("col", None, "row"),
            P("col", "row", None),
            P("col", "row", None),
        ),
        out_specs=(P(("row", "col"), None), P(("row", "col"), None), P("col", "row", None)),
        check_vma=False,
    )
```

```python
import functools

import jax
import jax.numpy as jnp
from jax import lax
from jax.experimental import pallas as pl
from jax.experimental.pallas import tpu as pltpu
from jax.sharding import PartitionSpec as P

BF = jnp.bfloat16
F32 = jnp.float32
CHUNKS = 2
SPLIT = 6


def swap(x, bits):
    n = lax.axis_size("row")
    return lax.ppermute(x, "row", [(i, i ^ bits) for i in range(n)])


def chain(x, chips=1, cross=0):
    n = lax.axis_size("row")
    hop = 4 * chips
    return lax.ppermute(
        x, "row", [(i, ((i + (hop if i % 2 == 0 else n - hop)) % n) ^ cross) for i in range(n)]
    )


def across(x, step, cross=0):
    n = lax.axis_size("col")
    return lax.ppermute(x, "col", [(i, ((i + 2 * step) % n) ^ cross) for i in range(n)])


def diagonal(x):
    rows, cols = lax.axis_size("row"), lax.axis_size("col")
    return lax.ppermute(
        x, ("row", "col"), [(r * cols + c, (r ^ 2) * cols + (c ^ 1)) for r in range(rows) for c in range(cols)]
    )


def leaf_kernel(place, parent, offset, z_ref, inv_ref, coup_ref, y_ref, *refs):
    up2, down2, up0, up1, down0, down1, own, z, inv, coup, y, acc, in_sem, out_sem = refs
    count = inv.shape[0]
    reads, writes = [], []
    for i in range(count):
        rows = pl.ds(i * 256, 256)
        reads.append(
            [
                pltpu.make_async_copy(inv_ref.at[i], inv.at[i], in_sem.at[3 * i]),
                pltpu.make_async_copy(z_ref.at[rows, :], z.at[rows, :], in_sem.at[3 * i + 1]),
                pltpu.make_async_copy(coup_ref.at[i], coup.at[i], in_sem.at[3 * i + 2]),
            ]
        )
        for copy in reads[i]:
            copy.start()
    acc[...] = jnp.zeros_like(acc)
    for i in range(count):
        for copy in reads[i]:
            copy.wait()
        rows = slice(i * 256, i * 256 + 256)
        solved = jnp.dot(inv[i], z[rows, :], preferred_element_type=F32).astype(BF)
        y[rows, :] = solved
        writes.append(
            pltpu.make_async_copy(
                y.at[pl.ds(i * 256, 256), :], y_ref.at[pl.ds(i * 256, 256), :], out_sem.at[i]
            )
        )
        writes[i].start()
        p = parent[i]
        away = ((p >> 1) - place[1]) & 3
        side = (p & 1) ^ place[2]
        acc[(away * 2 + offset[i]) * 2 + side] += jnp.dot(coup[i], solved, preferred_element_type=F32)
    up2[...] = acc[8:10].astype(BF)
    down2[...] = acc[10:12].astype(BF)
    own[...] = acc[0:4]
    up0[...] = acc[4:6].astype(BF)
    up1[...] = acc[6:8].astype(BF)
    down0[...] = acc[12:14].astype(BF)
    down1[...] = acc[14:16].astype(BF)
    for copy in writes:
        copy.wait()


def leaf_solve(place, z_leaf, leaf_inverse, coupling, parent, offset, targets):
    count, rows, _ = leaf_inverse.shape
    blk = coupling.shape[1]
    samples = z_leaf.shape[1]
    return pl.pallas_call(
        leaf_kernel,
        grid_spec=pltpu.PrefetchScalarGridSpec(
            num_scalar_prefetch=3,
            grid=(1,),
            in_specs=[pl.BlockSpec(memory_space=pl.ANY)] * 3,
            out_specs=[pl.BlockSpec(memory_space=pl.ANY)]
            + [pl.BlockSpec((2, blk, samples), lambda i, *_: (0, 0, 0))] * 6
            + [pl.BlockSpec((4, blk, samples), lambda i, *_: (0, 0, 0))],
            scratch_shapes=[
                pltpu.VMEM(z_leaf.shape, BF),
                pltpu.VMEM(leaf_inverse.shape, BF),
                pltpu.VMEM(coupling.shape, BF),
                pltpu.VMEM(z_leaf.shape, BF),
                pltpu.VMEM((targets, blk, samples), F32),
                pltpu.SemaphoreType.DMA((3 * count,)),
                pltpu.SemaphoreType.DMA((count,)),
            ],
        ),
        out_shape=[jax.ShapeDtypeStruct((count * rows, samples), BF)]
        + [jax.ShapeDtypeStruct((2, blk, samples), BF)] * 6
        + [jax.ShapeDtypeStruct((4, blk, samples), F32)],
        compiler_params=pltpu.CompilerParams(vmem_limit_bytes=24 << 20),
        cost_estimate=pl.CostEstimate(flops=810_000_000, bytes_accessed=8 << 20, transcendentals=0),
        name="leaf_solve",
    )(place, parent, offset, z_leaf, leaf_inverse, coupling)


def gather_kernel(own, from0, from1, back0, back1, z_ref, part_ref, mine_ref, rest_ref):
    for b, (f, g) in enumerate(((from0, back0), (from1, back1))):
        rows = slice(b * 128, b * 128 + 128)
        rest = z_ref[rows, :].astype(F32) - (own[2 * b] + f[0].astype(F32) + g[0].astype(F32))
        rest_ref[rows, :] = rest
        mine_ref[rows, :] = rest.astype(BF)
        part_ref[rows, :] = (own[2 * b + 1] + f[1].astype(F32) + g[1].astype(F32)).astype(BF)


def gather_x(own, from0, from1, back0, back1, z_sep):
    shape = z_sep.shape
    return pl.pallas_call(
        gather_kernel,
        out_shape=[
            jax.ShapeDtypeStruct(shape, BF),
            jax.ShapeDtypeStruct(shape, BF),
            jax.ShapeDtypeStruct(shape, F32),
        ],
        compiler_params=pltpu.CompilerParams(vmem_limit_bytes=16 << 20),
        cost_estimate=pl.CostEstimate(flops=2_000_000, bytes_accessed=4 << 20, transcendentals=0),
        name="gather_x",
    )(own, from0, from1, back0, back1, z_sep)


def pick_kernel(wanted, table, mask, factor, *refs):
    outs = refs[: len(wanted)]
    held, in_sem, out_sem = refs[len(wanted) :]
    jobs = []
    for o, groups in enumerate(wanted):
        order = [(m, j) for m, lo, hi in groups for j in range(lo, hi)]
        jobs += [(o, m, j, at) for at, (m, j) in enumerate(order)]
    reads, writes = [], []
    for i, (o, m, j, at) in enumerate(jobs):
        block = pl.multiple_of(table[m * 8 + j] * 256, 256)
        reads.append(pltpu.make_async_copy(factor.at[pl.ds(block, 256), :], held.at[i], in_sem.at[i]))
        reads[-1].start()
    for i, (o, m, j, at) in enumerate(jobs):
        reads[i].wait()
        keep = mask[table[m * 8 + j]].astype(F32)
        held[i] = (held[i].astype(F32) * keep).astype(BF)
        writes.append(
            pltpu.make_async_copy(held.at[i], outs[o].at[pl.ds(at * 256, 256), :], out_sem.at[i])
        )
        writes[-1].start()
    for copy in writes:
        copy.wait()


def pick(factor, table, mask, wanted):
    sizes = [sum(hi - lo for _, lo, hi in groups) for groups in wanted]
    total = sum(sizes)
    return pl.pallas_call(
        functools.partial(pick_kernel, wanted),
        grid_spec=pltpu.PrefetchScalarGridSpec(
            num_scalar_prefetch=2,
            grid=(1,),
            in_specs=[pl.BlockSpec(memory_space=pl.ANY)],
            out_specs=[pl.BlockSpec(memory_space=pl.ANY)] * len(wanted),
            scratch_shapes=[
                pltpu.VMEM((total, 256, 256), BF),
                pltpu.SemaphoreType.DMA((total,)),
                pltpu.SemaphoreType.DMA((total,)),
            ],
        ),
        out_shape=[jax.ShapeDtypeStruct((size * 256, 256), BF) for size in sizes],
        compiler_params=pltpu.CompilerParams(vmem_limit_bytes=60 << 20),
        cost_estimate=pl.CostEstimate(flops=total << 16, bytes_accessed=total << 18, transcendentals=0),
        name="pick_factor",
    )(table, mask, factor)


def sep_kernel(rest_ref, part_ref, near_ref, cross_ref, inv_ref, near_inv_ref, y_ref, pair_ref):
    mine = (rest_ref[...] - part_ref[...].astype(F32)).astype(BF)
    y = jnp.dot(inv_ref[0], mine, preferred_element_type=F32).astype(BF)
    y_ref[...] = y
    near = (near_ref[...].astype(F32) - cross_ref[...].astype(F32)).astype(BF)
    pair_ref[0:256, :] = y
    pair_ref[256:512, :] = jnp.dot(near_inv_ref[0], near, preferred_element_type=F32).astype(BF)


def sep_solve(rest, part, near, cross, sep_inverse, near_inverse):
    rows, samples = rest.shape
    return pl.pallas_call(
        sep_kernel,
        out_shape=[
            jax.ShapeDtypeStruct((rows, samples), BF),
            jax.ShapeDtypeStruct((2 * rows, samples), BF),
        ],
        compiler_params=pltpu.CompilerParams(vmem_limit_bytes=16 << 20),
        cost_estimate=pl.CostEstimate(flops=140_000_000, bytes_accessed=2 << 20, transcendentals=0),
        name="sep_solve",
    )(rest, part, near, cross, sep_inverse, near_inverse)


def multiply(f, y):
    total = jnp.dot(f[0][...], y[0][...], preferred_element_type=F32)
    for m in range(1, 4):
        total += jnp.dot(f[m][...], y[m][...], preferred_element_type=F32)
    return total


def start_kernel(*refs):
    refs[8][...] = multiply(refs[0:4], refs[4:8]).astype(BF)


def start(factors, first, blocks, panels, chunk, width):
    return pl.pallas_call(
        start_kernel,
        grid=(blocks,),
        in_specs=[pl.BlockSpec((256, 256), lambda i: (first + i, 0))] * 4
        + [pl.BlockSpec((256, width), lambda i, m=m: (m // 2, chunk)) for m in range(4)],
        out_specs=pl.BlockSpec((256, width), lambda i: (i, 0)),
        out_shape=jax.ShapeDtypeStruct((256 * blocks, width), BF),
        compiler_params=pltpu.CompilerParams(vmem_limit_bytes=16 << 20),
        cost_estimate=pl.CostEstimate(flops=blocks * 512 * 1024 * width, bytes_accessed=3 << 20, transcendentals=0),
        name="chain_start",
    )(*factors, *panels)


def middle_kernel(core, *refs):
    total = multiply(refs[0:4], refs[4:8]) + refs[8][...].astype(F32)
    total += jnp.where(pl.program_id(0) == core[0], refs[9][...].astype(F32), 0.0)
    refs[10][...] = total.astype(BF)


def middle(core, factors, first, panels, chunk, width, near, far):
    return pl.pallas_call(
        middle_kernel,
        grid_spec=pltpu.PrefetchScalarGridSpec(
            num_scalar_prefetch=1,
            grid=(2,),
            in_specs=[pl.BlockSpec((256, 256), lambda i, c: (first + i, 0))] * 4
            + [pl.BlockSpec((256, width), lambda i, c, m=m: (m // 2, chunk)) for m in range(4)]
            + [
                pl.BlockSpec((256, width), lambda i, c: (i, 0)),
                pl.BlockSpec((256, width), lambda i, c: (0, chunk)),
            ],
            out_specs=pl.BlockSpec((256, width), lambda i, c: (i, 0)),
        ),
        out_shape=jax.ShapeDtypeStruct((512, width), BF),
        compiler_params=pltpu.CompilerParams(vmem_limit_bytes=16 << 20),
        cost_estimate=pl.CostEstimate(flops=1024 * 1024 * width, bytes_accessed=3 << 20, transcendentals=0),
        name="chain_middle",
    )(core, *factors, *panels, near, far)


def last_kernel(core, *refs):
    total = (multiply(refs[0:4], refs[4:8]) + refs[8][...].astype(F32)).astype(BF)

    @pl.when(pl.program_id(0) == 0)
    def _():
        refs[9][...] = total

    @pl.when(pl.program_id(0) == 1)
    def _():
        refs[10][...] = total


def last(core, factors, first, panels, chunk, width, recv):
    return pl.pallas_call(
        last_kernel,
        grid_spec=pltpu.PrefetchScalarGridSpec(
            num_scalar_prefetch=1,
            grid=(2,),
            in_specs=[pl.BlockSpec((256, 256), lambda i, c, k=k: (k + (c[0] + i) % 2, 0)) for k in first]
            + [pl.BlockSpec((256, width), lambda i, c, m=m: (m // 2, chunk)) for m in range(4)]
            + [pl.BlockSpec((256, width), lambda i, c: ((c[0] + i) % 2, 0))],
            out_specs=[pl.BlockSpec((256, width), lambda i, c: (0, 0))] * 2,
        ),
        out_shape=[jax.ShapeDtypeStruct((256, width), BF)] * 2,
        compiler_params=pltpu.CompilerParams(vmem_limit_bytes=16 << 20),
        cost_estimate=pl.CostEstimate(flops=1024 * 1024 * width, bytes_accessed=3 << 20, transcendentals=0),
        name="chain_last",
    )(core, *factors, *panels, recv)


def own_kernel(*refs):
    refs[9][...] = refs[8][...].astype(F32) - multiply(refs[0:4], refs[4:8])


def own_rows(factors, first, panels, z_top):
    samples = z_top.shape[1]
    return pl.pallas_call(
        own_kernel,
        grid=(1,),
        in_specs=[pl.BlockSpec((256, 256), lambda i, k=k: (k, 0)) for k in first]
        + [pl.BlockSpec((256, samples), lambda i, m=m: (m // 2, 0)) for m in range(4)]
        + [pl.BlockSpec((256, samples), lambda i: (0, 0))],
        out_specs=pl.BlockSpec((256, samples), lambda i: (0, 0)),
        out_shape=jax.ShapeDtypeStruct((256, samples), F32),
        compiler_params=pltpu.CompilerParams(vmem_limit_bytes=16 << 20),
        cost_estimate=pl.CostEstimate(flops=512 * 1024 * samples, bytes_accessed=3 << 20, transcendentals=0),
        name="own_rows",
    )(*factors, *panels, z_top)


def shards(
    z_leaf,
    leaf_inverse,
    lower_separator_coupling,
    leaf_parent,
    leaf_offset,
    z_sep,
    sep_inverse,
    top_factor,
    reader_mask,
    z_top,
):
    columns = lax.axis_size("col")
    samples = z_sep.shape[1]
    me = lax.axis_index("row").astype(jnp.int32)
    core = me % 2
    table = []
    for m in range(4):
        peer = me ^ m
        sign = 1 - 2 * (peer % 2)
        base = me // 4
        pair = (peer // 2) % 2
        side = peer % 2

        def block(z, k):
            return ((z + 16) % 8) * 4 + pair * 2 + k

        table.append(block(base + 4, side))
        for d in (3, 2):
            for k in (0, 1):
                table.append(block(base + d * sign, k))
        table.append(block(base, side))
        for k in (0, 1):
            table.append(block(base + sign, k))
    table = jnp.stack(table).astype(jnp.int32)
    mask = reader_mask[0, 0]

    col = lax.axis_index("col").astype(jnp.int32)
    where = jnp.stack([me, col >> 1, col & 1])
    near_f, far_a = pick(
        top_factor[0], table, mask, (((1, 0, 8),), ((2, 0, SPLIT), (3, 0, SPLIT)))
    )
    near_inverse = swap(sep_inverse, 2)
    z_leaf, near_f, far_a, near_inverse = lax.optimization_barrier((z_leaf, near_f, far_a, near_inverse))
    far_a = swap(far_a, 2)
    near_f = swap(near_f, 1)
    y_leaf, up2, down2, up0, up1, down0, down1, own = leaf_solve(
        where, z_leaf, leaf_inverse, lower_separator_coupling, leaf_parent, leaf_offset, 2 * columns
    )
    from2, back2 = across(up2, 1), across(down2, 3)
    from1, back0 = across(up1, 1), across(down0, 3)
    own_f, far_b, cross_b = pick(
        top_factor[0], table, mask, (((0, 0, 8),), ((2, SPLIT, 8),), ((3, SPLIT, 8),))
    )
    from1, near_f, far_a, own_f, far_b, cross_b, near_inverse = lax.optimization_barrier(
        (from1, near_f, far_a, own_f, far_b, cross_b, near_inverse)
    )
    cross_a = swap(far_a[SPLIT * 256 :], 1)
    from0 = across((up0.astype(F32) + from2.astype(F32)).astype(BF), 1)
    back1 = across((down1.astype(F32) + back2.astype(F32)).astype(BF), 3)
    part, mine, rest = gather_x(own, from0, from1, back0, back1, z_sep)
    theirs, cross, near = across(part, 0, 1), diagonal(part), swap(mine, 2)
    y_sep, pair = sep_solve(rest, theirs, near, cross, sep_inverse, near_inverse)
    pair_core = swap(pair, 1)
    pair_core, far_b, cross_b = lax.optimization_barrier((pair_core, far_b, cross_b))
    far_b, cross_b = swap(far_b, 2), swap(cross_b, 3)
    first_f = [own_f, near_f, far_a, cross_a]
    last_f = [own_f, near_f, far_b, cross_b]
    skip = (SPLIT, SPLIT, 0, 0)
    panels = [pair, pair_core, pair, pair_core]

    core_id = core.reshape(1)
    width = samples // CHUNKS
    far = chain(start(first_f, 0, 1, panels, 0, samples), 2)
    arrived = [chain(start(first_f, 1, 2, panels, c, width)) for c in range(CHUNKS)]
    for c in range(CHUNKS):
        arrived[c] = chain(middle(core_id, first_f, 3, panels, c, width, arrived[c], far))
    for c in range(CHUNKS):
        same, other = last(core_id, last_f, skip, panels, c, width, arrived[c])
        arrived[c] = (chain(same), chain(other, 1, 1))
    rest = own_rows(first_f, [5] * 4, panels, z_top[0])
    tops = [
        rest[:, c * width : (c + 1) * width] - (arrived[c][0].astype(F32) + arrived[c][1].astype(F32))
        for c in range(CHUNKS)
    ]
    top_rhs = jnp.concatenate(tops, axis=1)
    return y_leaf, y_sep, top_rhs[None]


def solution(mesh):
    return jax.shard_map(
        shards,
        mesh=mesh,
        in_specs=(
            P(("row", "col"), None),
            P(("row", "col"), None, None),
            P(("row", "col"), None, None),
            P(("row", "col")),
            P(("row", "col")),
            P(("row", "col"), None),
            P(("row", "col"), None, None),
            P("col", None, "row"),
            P("col", "row", None),
            P("col", "row", None),
        ),
        out_specs=(P(("row", "col"), None), P(("row", "col"), None), P("col", "row", None)),
        check_vma=False,
    )
```
